128 devices in a mesh: sec: 2 (over core), op: 64 (over z, y, x).
Axes of the slice: x: 4, y: 4, z: 4, core: 2. Of those that a mesh axis runs over, the one named last changes fastest.
Arguments:
- wavefunction: bfloat16 [24, 512, 512], P('sec'), may hold values from -6 to 6
- live_rows: int32 [24], P('sec'), may hold values from 64 to 512, as said below
- left_env: bfloat16 [128, 24, 512, 512], P('op', 'sec'), may hold values from -0.75 to 0.75
- right_env: bfloat16 [128, 24, 512, 512], P('op', 'sec'), may hold values from -0.0234375 to 0.0234375
- routes: int32 [128, 24], P('op', 'sec'), may hold values from 0 to 23, as said below
Outputs:
- sigma_blocks: bfloat16 [24, 512, 512], P('sec', 'op')
The draws below stay inside these ranges and needn't reach their ends.
Inputs may be any that keep to these rules, and one draw needn't show every extreme that they name: `live_rows`: multiples of 64; some sector has 512. For each term, routes[t] maps the 24 sectors one to one onto the 24 sectors. Sector j stands on index j // 12 of sec. Over the 2 terms of one index of op, at most 13 blocks go from one index of sec to one index of sec, and some pair reaches 13.
All inputs are finite; a program needn't handle non-finite values.
Results may differ from the reference program's by a relative error of at most 0.0049.
Values may be sent and summed in bfloat16 or wider, within the bound.
No kernel may reach another device: no remote copies, remote signals or barrier semaphores. Data moves between devices by JAX's collectives and lax.ppermute only.
A program may use at most 192 MiB of HBM per device.

```python
import jax
import jax.numpy as jnp
from jax import lax

BLOCK = 512
PAD = 64
S_DEV = 12
TERMS_DEV = 2
SECTORS = 24
TERMS = 128


def route_group(key, sec_count):
    key_order, key_moves, key_shuffle, key_local = jax.random.split(key, 4)
    item_count = TERMS_DEV * S_DEV
    per_pair = item_count // sec_count
    order = jax.random.permutation(key_order, sec_count)
    moves = jax.random.randint(key_moves, (), 1, sec_count // 2 + 1)
    active = (jnp.arange(sec_count // 2) < moves).astype(jnp.int32)
    counts = jnp.full((sec_count,), per_pair, jnp.int32)
    counts = counts.at[order[0::2]].add(active).at[order[1::2]].add(-active)
    bounds = jnp.cumsum(counts)
    sorted_offset = jnp.sum((bounds[None, :] <= jnp.arange(item_count)[:, None]).astype(jnp.int32), axis=1)
    shuffle = jax.random.permutation(key_shuffle, item_count)
    offsets = sorted_offset[shuffle].reshape(TERMS_DEV, S_DEV)
    local_keys = jax.random.split(key_local, TERMS_DEV)
    local_slot = jax.vmap(lambda single_key: jax.random.permutation(single_key, S_DEV))(local_keys)
    device = jnp.arange(sec_count)
    dest_device = (device[None, :, None] + offsets[:, None, :]) % sec_count
    destination = dest_device * S_DEV + local_slot[:, None, :]
    return destination.reshape(TERMS_DEV, sec_count * S_DEV)


def draw_routes(key, part):
    key = jax.random.fold_in(key, 11)
    sec_count = SECTORS // S_DEV
    op_count = TERMS // TERMS_DEV
    group_keys = jax.random.split(key, op_count)
    grouped = jax.vmap(lambda single_key: route_group(single_key, sec_count))(group_keys)
    return grouped.reshape(TERMS, SECTORS).astype(jnp.int32)


def draw_live_rows(key, part):
    key = jax.random.fold_in(key, 5)
    key_size, key_spot = jax.random.split(key)
    levels = jax.random.randint(key_size, (SECTORS,), 1, BLOCK // PAD + 1)
    widest = jax.random.randint(key_spot, (), 0, SECTORS)
    levels = jnp.where(jnp.arange(SECTORS) == widest, BLOCK // PAD, levels)
    return (levels * PAD).astype(jnp.int32)


def with_spikes(entries, stream_key, source, target, parts, factor):
    def block_of(dim):
        return (jnp.arange(entries.shape[dim]) // (entries.shape[dim] // parts)).reshape((-1,) + (1,) * (entries.ndim - 1 - dim))

    near = jax.random.permutation(stream_key, parts)[block_of(target)]
    other_side = (block_of(target) + parts // 2) % parts
    return jnp.where((block_of(source) == near) | (block_of(source) == other_side), factor * entries, entries)


def steps_of(own_key, extent, cuts, least, top_value):
    level, own = 1.0, jax.random.fold_in(own_key, 6)
    for axis_at, parts in cuts:
        heights = jnp.exp(jax.random.uniform(jax.random.fold_in(own, axis_at), (parts,), jnp.float32, least / len(cuts), top_value / len(cuts)))
        level = level * jnp.repeat(heights, extent[axis_at] // parts).reshape([-1 if axis == axis_at else 1 for axis in range(len(extent))])
    return level


def gaussian(own_key, extent, scale, reach, cuts=(), kind=jnp.bfloat16):
    array = scale * jax.random.normal(own_key, extent, jnp.float32)
    if cuts:
        array = array * steps_of(own_key, extent, cuts, -0.22, 0.18)
    return jnp.clip(array, -reach, reach).astype(kind)


def heavy_noise(stream_key, dims, scale, reach, cuts, heavy, held_as=jnp.bfloat16):
    entries = scale * jax.random.normal(stream_key, dims, jnp.float32)
    if cuts:
        entries = entries * steps_of(stream_key, dims, cuts, -0.22, 0.18)
    return jnp.clip(with_spikes(entries, jax.random.fold_in(stream_key, 3), *heavy), -reach, reach).astype(held_as)


def setup_inputs(seed: int = 0) -> dict:
    key_of = jax.random.split(jax.random.key(seed), 6)
    return {
        "wavefunction": gaussian(key_of[0], (SECTORS, BLOCK, BLOCK), 1.0, 6.0, ((0, 2),)),
        "live_rows": draw_live_rows(jax.random.fold_in(key_of[5], 71), 0),
        "left_env": heavy_noise(key_of[2], (TERMS, SECTORS, BLOCK, BLOCK), BLOCK ** -0.5, 0.75, ((0, 64), (1, 2)), (0, 2, 64, 4.0)),
        "right_env": gaussian(key_of[3], (TERMS, SECTORS, BLOCK, BLOCK), (BLOCK * TERMS) ** -0.5, 0.0234375, ((0, 64), (1, 2))),
        "routes": draw_routes(jax.random.fold_in(key_of[5], 71), 0),
    }


def reference(wavefunction, live_rows, left_env, right_env, routes):
    row_index = jnp.arange(BLOCK, dtype=jnp.int32)
    kept_rows = row_index[None, :, None] < live_rows[:, None, None]
    psi_live = jnp.where(kept_rows, wavefunction, jnp.zeros_like(wavefunction)).astype(jnp.float32)
    term_index = jnp.broadcast_to(jnp.arange(TERMS, dtype=jnp.int32)[:, None], routes.shape)
    sector_index = jnp.broadcast_to(jnp.arange(SECTORS, dtype=jnp.int32)[None, :], routes.shape)
    source_sector = jnp.zeros((TERMS, SECTORS), jnp.int32).at[term_index, routes].set(sector_index)

    def one_term(running_sum, inputs):
        left_block, right_block, source_row = inputs
        mixed = jnp.einsum('jab,jbc->jac', left_block.astype(jnp.float32), psi_live).astype(jnp.bfloat16)
        chosen = jnp.take(mixed, source_row, axis=0).astype(jnp.float32)
        running_sum = running_sum + jnp.einsum('sab,sbc->sac', chosen, right_block.astype(jnp.float32))
        return running_sum, None

    start_sum = jnp.zeros((SECTORS, BLOCK, BLOCK), jnp.float32)
    final_sum, unused_out = lax.scan(one_term, start_sum, (left_env, right_env, source_sector))
    return final_sum.astype(jnp.bfloat16)
```

```python
import functools

import jax
import jax.numpy as jnp
from jax import lax
from jax.experimental import pallas as pl
from jax.experimental.pallas import tpu as pltpu
from jax.sharding import PartitionSpec as P

BF16, F32, I32 = jnp.bfloat16, jnp.float32, jnp.int32
PARTS = 3
ORDERS = ((0, 1, 2), (1, 2, 0), (2, 0, 1))
STRIDES = (16, 4, 1)
SMEM_SPEC = pl.BlockSpec(memory_space=pltpu.SMEM)
VMEM_SPEC = pl.BlockSpec(memory_space=pltpu.VMEM)
ANY_SPEC = pl.BlockSpec(memory_space=pl.ANY)


def invert_routes(routes, inverse):
    terms, slots = routes.shape
    for t in range(terms):
        for s in range(inverse.shape[1]):
            inverse[t, s] = -1
    for t in range(terms):
        for j in range(slots):
            inverse[t, routes[t, j]] = j


def list_items(inverse, owner, first, last, slots, item_t, item_j, item_s):
    count = jnp.int32(0)
    for s in range(first, last):
        for t in range(inverse.shape[0]):
            j = inverse[t, owner * slots + s]
            item_t[count] = t
            item_j[count] = j
            item_s[count] = s
            count = count + (j >= 0).astype(I32)
    return count


def masked(psi, live):
    rows = lax.broadcasted_iota(I32, psi.shape, 0)
    return jnp.where(rows < live, psi, jnp.zeros_like(psi))


def dot(a, b):
    return jnp.dot(a, b, preferred_element_type=F32)


def export_kernel(
    routes, live, psi, left, out, inverse, item_t, item_j, item_s, psi_buf, left_buf, out_buf, in_sem, out_sem
):
    slots = psi.shape[0]
    other = 1 - lax.axis_index("sec")
    invert_routes(routes, inverse)
    count = list_items(inverse, other, 0, slots, slots, item_t, item_j, item_s)

    def loads(i):
        j = item_j[i]
        return (
            pltpu.make_async_copy(left.at[item_t[i], j], left_buf.at[i], in_sem.at[0, i]),
            pltpu.make_async_copy(psi.at[j], psi_buf.at[i], in_sem.at[1, i]),
        )

    def store(i):
        return pltpu.make_async_copy(out_buf.at[i], out.at[i], out_sem.at[i])

    @pl.loop(0, count)
    def _(i):
        for copy in loads(i):
            copy.start()

    @pl.loop(0, count)
    def _(i):
        for copy in loads(i):
            copy.wait()
        out_buf[i] = dot(left_buf[i], masked(psi_buf[i], live[item_j[i]])).astype(BF16)
        store(i).start()

    @pl.loop(0, count)
    def _(i):
        store(i).wait()


def local_kernel(
    routes, live, psi, left, right, *refs
):
    sums = refs[:PARTS]
    inverse, item_t, item_j, item_s, psi_buf, left_buf, right_buf, sem = refs[PARTS:]
    slots = psi.shape[0]
    terms = left.shape[0]
    me = lax.axis_index("sec")
    invert_routes(routes, inverse)
    count = list_items(inverse, me, 0, slots, slots, item_t, item_j, item_s)

    def loads(i):
        t, j = item_t[i], item_j[i]
        return (
            pltpu.make_async_copy(left.at[t, j], left_buf.at[i], sem.at[0, i]),
            pltpu.make_async_copy(psi.at[j], psi_buf.at[i], sem.at[1, i]),
            pltpu.make_async_copy(right.at[t, item_s[i]], right_buf.at[i], sem.at[2, i]),
        )

    @pl.loop(0, count)
    def _(i):
        for copy in loads(i):
            copy.start()

    per_part = slots // PARTS
    for p in range(PARTS):
        for k in range(per_part):
            s = me * slots + p * per_part + k
            none = inverse[0, s] < 0
            for t in range(1, terms):
                none = jnp.logical_and(none, inverse[t, s] < 0)

            @pl.when(none)
            def _():
                sums[p][k] = jnp.zeros(sums[p].shape[1:], F32)

    @pl.loop(0, count)
    def _(i):
        for copy in loads(i):
            copy.wait()
        mixed = dot(left_buf[i], masked(psi_buf[i], live[item_j[i]])).astype(BF16)
        product = dot(mixed, right_buf[i])
        s = item_s[i]
        again = jnp.logical_and(i > 0, item_s[jnp.maximum(i - 1, 0)] == s)
        for p in range(PARTS):

            @pl.when(jnp.logical_and(s >= p * per_part, s < (p + 1) * per_part))
            def _():
                k = s - p * per_part
                sums[p][k] = jnp.where(again, sums[p][k], 0.0) + product


def ring_places(c, core):
    near, far = c ^ 1, 3 - c
    return (c, jnp.where(core == 0, far, near), jnp.where(core == 0, near, far), c ^ 2)


def remote_kernel(
    part, order, routes, received, right, base, send, keep, inverse, item_t, item_j, item_s, mix_buf, right_buf, total, sem
):
    slots = right.shape[1]
    terms = right.shape[0]
    per_part = base.shape[0]
    first = part * per_part
    me = lax.axis_index("sec")
    op = lax.axis_index("op")
    invert_routes(routes, inverse)
    ahead = jnp.int32(0)
    for s in range(first):
        for t in range(terms):
            ahead = ahead + (inverse[t, me * slots + s] >= 0).astype(I32)
    count = list_items(inverse, me, first, first + per_part, slots, item_t, item_j, item_s)

    def loads(i):
        return (
            pltpu.make_async_copy(received.at[ahead + i], mix_buf.at[i], sem.at[0, i]),
            pltpu.make_async_copy(right.at[item_t[i], item_s[i]], right_buf.at[i], sem.at[1, i]),
        )

    @pl.loop(0, count)
    def _(i):
        for copy in loads(i):
            copy.start()

    for k in range(per_part):
        none = inverse[0, me * slots + first + k] < 0
        for t in range(1, terms):
            none = jnp.logical_and(none, inverse[t, me * slots + first + k] < 0)

        @pl.when(none)
        def _():
            total[k] = base[k]

    @pl.loop(0, count)
    def _(i):
        for copy in loads(i):
            copy.wait()
        s = item_s[i]
        k = s - first
        again = jnp.logical_and(i > 0, item_s[jnp.maximum(i - 1, 0)] == s)
        total[k] = jnp.where(again, total[k], base[k]) + dot(mix_buf[i], right_buf[i])

    place = (op // 16, (op // 4) % 4, op % 4)
    rings = [[8 * STRIDES[a] * spot for spot in ring_places(place[a], me)] for a in order]
    half = keep.shape[0]
    for n in range(2 * half):
        row = pl.multiple_of(rings[0][n // 16] + rings[1][n // 4 % 4] + rings[2][n % 4], 8)
        rows = jnp.concatenate([total[k, pl.ds(row, 8), :] for k in range(per_part)], axis=0)
        if n < half:
            keep[n] = rows
        else:
            send[n - half] = rows.astype(BF16)


def partner_lists():
    lists = []
    for stride in STRIDES:
        pair = []
        for step in range(2):
            perm = []
            for core in range(2):
                for op in range(64):
                    c = op // stride % 4
                    d = c ^ 1 if core == step else 3 - c
                    perm.append((core * 64 + op, core * 64 + op + (d - c) * stride))
            pair.append(perm)
        lists.append(pair)
    return lists


def per_device(psi, live, left, right, routes):
    slots, rows, cols = psi.shape
    terms = left.shape[0]
    items = terms * slots
    capacity = items // 2 + 1
    per_part = slots // PARTS
    part_items = terms * per_part
    lists = [
        pltpu.SMEM((terms, 2 * slots), I32),
        pltpu.SMEM((items + 1,), I32),
        pltpu.SMEM((items + 1,), I32),
        pltpu.SMEM((items + 1,), I32),
    ]
    block = (rows, cols)
    half = 32
    other_routes = lax.ppermute(routes, "sec", [(0, 1), (1, 0)])
    flops = 2 * rows * rows * cols

    outgoing = pl.pallas_call(
        export_kernel,
        out_shape=jax.ShapeDtypeStruct((capacity,) + block, BF16),
        in_specs=[SMEM_SPEC, SMEM_SPEC, ANY_SPEC, ANY_SPEC],
        out_specs=ANY_SPEC,
        scratch_shapes=lists
        + [pltpu.VMEM((capacity,) + block, BF16)] * 3
        + [pltpu.SemaphoreType.DMA((2, capacity)), pltpu.SemaphoreType.DMA((capacity,))],
        compiler_params=pltpu.CompilerParams(vmem_limit_bytes=32 << 20),
        cost_estimate=pl.CostEstimate(flops=capacity * flops, bytes_accessed=capacity * 3 << 19, transcendentals=0),
        name="export_mixed",
    )(routes, live, psi, left)
    received = lax.ppermute(outgoing, "sec", [(0, 1), (1, 0)])

    bases = pl.pallas_call(
        local_kernel,
        out_shape=[pltpu.VMEM((per_part,) + block, F32)] * PARTS,
        in_specs=[SMEM_SPEC, SMEM_SPEC, ANY_SPEC, ANY_SPEC, ANY_SPEC],
        out_specs=[VMEM_SPEC] * PARTS,
        scratch_shapes=lists
        + [pltpu.VMEM((capacity,) + block, BF16)] * 3
        + [pltpu.SemaphoreType.DMA((3, capacity))],
        compiler_params=pltpu.CompilerParams(vmem_limit_bytes=44 << 20),
        cost_estimate=pl.CostEstimate(flops=2 * capacity * flops, bytes_accessed=capacity * 3 << 19, transcendentals=0),
        name="local_sum",
    )(routes, live, psi, left, right)

    partners = partner_lists()
    kept, coming = [], []
    for part in range(PARTS):
        send, keep = pl.pallas_call(
            functools.partial(remote_kernel, part, ORDERS[part]),
            out_shape=[
                jax.ShapeDtypeStruct((half, per_part * 8, cols), BF16),
                jax.ShapeDtypeStruct((half, per_part * 8, cols), F32),
            ],
            in_specs=[SMEM_SPEC, ANY_SPEC, ANY_SPEC, VMEM_SPEC],
            out_specs=[VMEM_SPEC, VMEM_SPEC],
            scratch_shapes=lists
            + [pltpu.VMEM((part_items,) + block, BF16)] * 2
            + [pltpu.VMEM((per_part,) + block, F32), pltpu.SemaphoreType.DMA((2, part_items))],
            compiler_params=pltpu.CompilerParams(vmem_limit_bytes=32 << 20),
            cost_estimate=pl.CostEstimate(flops=part_items * flops, bytes_accessed=part_items * 1 << 20, transcendentals=0),
            name="remote_sum",
        )(other_routes, received, right, bases[part])
        kept.append(keep)
        coming.append(lax.ppermute(send, ("sec", "op"), partners[ORDERS[part][0]][0]))

    for step in range(1, 6):
        half //= 2
        for part in range(PARTS):
            keep, come = kept[part], coming[part]
            send = (keep[half:] + come[half:].astype(F32)).astype(BF16)
            kept[part] = keep[:half] + come[:half].astype(F32)
            axis = ORDERS[part][step // 2]
            coming[part] = lax.ppermute(send, ("sec", "op"), partners[axis][step % 2])
    done = [(keep + come.astype(F32)).astype(BF16) for keep, come in zip(kept, coming)]
    return jnp.concatenate([d.reshape(per_part, 8, cols) for d in done], axis=0)


def solution(mesh):
    placed = (
        P("sec", None, None),
        P("sec"),
        P("op", "sec", None, None),
        P("op", "sec", None, None),
        P("op", "sec"),
    )
    return jax.shard_map(
        per_device, mesh=mesh, in_specs=placed, out_specs=P("sec", "op", None), check_vma=False
    )
```

```python
import functools

import jax
import jax.numpy as jnp
from jax import lax
from jax.experimental import pallas as pl
from jax.experimental.pallas import tpu as pltpu
from jax.sharding import PartitionSpec as P

BF16, F32, I32 = jnp.bfloat16, jnp.float32, jnp.int32
PARTS = 3
PAD = 64
LIST, EXPORT, LOCAL, HERE, SLOT, PLAN = 32, 0, 64, 128, 160, 192
ORDERS = ((0, 1, 2), (1, 2, 0), (2, 0, 1))
STRIDES = (16, 4, 1)
SMEM_SPEC = pl.BlockSpec(memory_space=pltpu.SMEM)
VMEM_SPEC = pl.BlockSpec(memory_space=pltpu.VMEM)
ANY_SPEC = pl.BlockSpec(memory_space=pl.ANY)
HBM_SPEC = pl.BlockSpec(memory_space=pltpu.HBM)


def dot(a, b):
    return jnp.dot(a, b, preferred_element_type=F32)


def cleared(psi_live, j, live):
    rows, cols = psi_live.shape[1:]

    @pl.loop(live // PAD, rows // PAD)
    def _(n):
        psi_live[j, pl.ds(pl.multiple_of(n * PAD, PAD), PAD), :] = jnp.zeros((PAD, cols), BF16)


def waited(source, target, sem):
    @pl.loop(0, target.shape[0])
    def _(i):
        pltpu.make_async_copy(source.at[0, 0], target.at[i], sem.at[i]).wait()


def first_kernel(
    routes_in, live_in, psi, left, out, psi_live, ahead, plan, routes, live, inverse, state, left_buf,
    table_sem, psi_sem, left_sem, ahead_sem
):
    terms, slots = routes.shape
    me = lax.axis_index("sec")
    tables = (
        pltpu.make_async_copy(routes_in, routes, table_sem.at[0]),
        pltpu.make_async_copy(live_in, live, table_sem.at[1]),
    )
    for copy in tables:
        copy.start()

    quarter = psi.shape[1] // 4

    def load_psi(j, q):
        piece = pl.ds(quarter * q, quarter)
        return pltpu.make_async_copy(psi.at[j, piece, :], psi_live.at[j, piece, :], psi_sem.at[j, q])

    def each_live_quarter(j, do):
        for q in range(4):
            pl.when(live[j] > quarter * q)(functools.partial(do, j, q))

    def want_psi(j):
        @pl.when(state[j] == 0)
        def _():
            each_live_quarter(j, lambda j, q: load_psi(j, q).start())
            state[j] = 1

    def have_psi(j):
        @pl.when(state[j] == 1)
        def _():
            each_live_quarter(j, lambda j, q: load_psi(j, q).wait())
            cleared(psi_live, j, live[j])
            state[j] = 2

    for j in range(slots):
        state[j] = 0
    for t in range(terms):
        for s in range(2 * slots):
            inverse[t, s] = -1
    for copy in tables:
        copy.wait()
    for t in range(terms):
        for j in range(slots):
            inverse[t, routes[t, j]] = j

    def listed(owner, at):
        count = jnp.int32(0)
        for s in range(slots):
            for t in range(terms):
                j = inverse[t, owner * slots + s]
                plan[at + count] = t
                plan[at + LIST + count] = j
                count = count + (j >= 0).astype(I32)
        for n in range(11, 13):
            plan[at + n] = jnp.where(n < count, plan[at + n], plan[at + 10])
            plan[at + LIST + n] = jnp.where(n < count, plan[at + LIST + n], plan[at + LIST + 10])

    first = out.shape[0]
    listed(1 - me, EXPORT)

    def load_left(i):
        source = left.at[plan[EXPORT + i], plan[EXPORT + LIST + i]]
        return pltpu.make_async_copy(source, left_buf.at[i], left_sem.at[i])

    @pl.loop(0, first)
    def _(i):
        want_psi(plan[EXPORT + LIST + i])
        load_left(i).start()

    @pl.loop(0, slots)
    def _(j):
        want_psi(j)

    listed(me, LOCAL)

    @pl.loop(0, ahead.shape[0])
    def _(i):
        at = EXPORT + first + i
        pltpu.make_async_copy(left.at[plan[at], plan[at + LIST]], ahead.at[i], ahead_sem.at[i]).start()

    local_count = jnp.int32(0)
    other_count = jnp.int32(0)
    for s in range(slots):
        for t in range(terms):
            here = (inverse[t, me * slots + s] >= 0).astype(I32)
            plan[HERE + terms * s + t] = here
            plan[SLOT + terms * s + t] = jnp.where(here == 1, local_count, other_count)
            local_count = local_count + here
            other_count = other_count + 1 - here
    for group in (range(first // 2), range(first // 2, first)):
        for i in group:
            have_psi(plan[EXPORT + LIST + i])
            load_left(i).wait()
        for i in group:
            out[i] = dot(left_buf[i], psi_live[plan[EXPORT + LIST + i]]).astype(BF16)
    for j in range(slots):
        have_psi(j)
    waited(left, ahead, ahead_sem)


def last_kernel(plan, psi_live, ahead, left, out, left_local, sem):
    count = out.shape[0]

    @pl.loop(0, left_local.shape[0])
    def _(i):
        at = LOCAL + i
        pltpu.make_async_copy(left.at[plan[at], plan[at + LIST]], left_local.at[i], sem.at[i]).start()

    for i in range(count):
        out[i] = dot(ahead[i], psi_live[plan[EXPORT + LIST + 13 - count + i]]).astype(BF16)
    waited(left, left_local, sem)


def load_right(right, part, target, sem):
    terms, _, rows, _ = right.shape
    per_part = target.shape[0]

    def load(k, t):
        source = right.at[t, part * per_part + k]
        return pltpu.make_async_copy(source, target.at[k, pl.ds(rows * t, rows), :], sem.at[k, t])

    @pl.loop(0, per_part)
    def _(k):
        for t in range(terms):
            load(k, t).start()

    def wait():
        @pl.loop(0, per_part)
        def _(k):
            for t in range(terms):
                load(k, t).wait()

    return wait


def local_kernel(plan, psi_live, left_local, right, out, right_part, sem):
    wait = load_right(right, 0, right_part, sem)
    for i in range(out.shape[0]):
        out[i] = dot(left_local[i], psi_live[plan[LOCAL + LIST + i]]).astype(BF16)
    wait()


def ring_places(c, core):
    near, far = c ^ 1, 3 - c
    return (c, jnp.where(core == 0, far, near), jnp.where(core == 0, near, far), c ^ 2)


def part_kernel(part, order, *refs):
    if part < PARTS - 1:
        plan, local_mixed, *received, right_part, right, send, keep, right_next, total, mixed, sem = refs
        wait = load_right(right, part + 1, right_next, sem)
    else:
        plan, local_mixed, *received, right_part, send, keep, total, mixed = refs
    per_part, rows, _ = total.shape
    terms = right_part.shape[1] // rows
    me = lax.axis_index("sec")
    op = lax.axis_index("op")
    place = (op // 16, (op // 4) % 4, op % 4)
    rings = [[8 * STRIDES[a] * spot for spot in ring_places(place[a], me)] for a in order]
    half = keep.shape[0]

    def block(s, t):
        here, slot = plan[HERE + terms * s + t], plan[SLOT + terms * s + t]
        last = received[0].shape[0] - 1
        came = received[0][jnp.minimum(slot, last)]
        if len(received) > 1:
            came = jnp.where(slot > last, received[1][jnp.clip(slot - last - 1, 0, received[1].shape[0] - 1)], came)
        return jnp.where(here == 1, local_mixed[slot], came)

    for k in range(per_part):
        s = part * per_part + k
        for t in range(terms):
            mixed[k, :, rows * t : rows * (t + 1)] = block(s, t)
        total[k] = dot(mixed[k], right_part[k])
    for pair in range(per_part // 2):
        for n in range(2 * half):
            row = pl.multiple_of(rings[0][n // 16] + rings[1][n // 4 % 4] + rings[2][n % 4], 8)
            piece = jnp.concatenate([total[2 * pair + e, pl.ds(row, 8), :] for e in range(2)], axis=0)
            if n < half:
                keep[n, pl.ds(16 * pair, 16), :] = piece
            else:
                send[n - half, pl.ds(16 * pair, 16), :] = piece.astype(BF16)
    if part < PARTS - 1:
        wait()


def partner_lists():
    lists = []
    for stride in STRIDES:
        pair = []
        for step in range(2):
            perm = []
            for core in range(2):
                for op in range(64):
                    c = op // stride % 4
                    d = c ^ 1 if core == step else 3 - c
                    perm.append((core * 64 + op, core * 64 + op + (d - c) * stride))
            pair.append(perm)
        lists.append(pair)
    return lists


def per_device(psi, live, left, right, routes):
    slots, rows, cols = psi.shape
    terms = left.shape[0]
    items = terms * slots
    capacity = items // 2 + 1
    per_part = slots // PARTS
    part_items = terms * per_part
    psi, live, left, right, routes = (
        pltpu.with_memory_space_constraint(x, pltpu.HBM) for x in (psi, live, left, right, routes)
    )
    block = (rows, cols)
    half = 32
    swap = [(0, 1), (1, 0)]
    flops = 2 * rows * rows * cols
    first, last = part_items, capacity - part_items

    def cost(dots, blocks):
        return pl.CostEstimate(flops=dots * flops, bytes_accessed=blocks * rows * cols * 2, transcendentals=0)

    def blocks(*count):
        return pltpu.VMEM(count + block, BF16)

    def params(mib):
        return pltpu.CompilerParams(vmem_limit_bytes=mib << 20)

    outgoing, psi_live, ahead, plan = pl.pallas_call(
        first_kernel,
        out_shape=[blocks(first), blocks(slots), blocks(last), pltpu.SMEM((PLAN,), I32)],
        in_specs=[HBM_SPEC] * 4,
        out_specs=[VMEM_SPEC] * 3 + [SMEM_SPEC],
        scratch_shapes=[
            pltpu.SMEM((terms, slots), I32),
            pltpu.SMEM((slots,), I32),
            pltpu.SMEM((terms, 2 * slots), I32),
            pltpu.SMEM((slots,), I32),
            blocks(first),
            pltpu.SemaphoreType.DMA((2,)),
            pltpu.SemaphoreType.DMA((slots, 4)),
            pltpu.SemaphoreType.DMA((first,)),
            pltpu.SemaphoreType.DMA((last,)),
        ],
        compiler_params=params(8),
        cost_estimate=cost(first, 2 * capacity),
        name="first_exports",
    )(routes, live, psi, left)
    received = [lax.ppermute(outgoing, "sec", swap)]

    outgoing, left_local = pl.pallas_call(
        last_kernel,
        out_shape=[blocks(last), blocks(capacity)],
        in_specs=[SMEM_SPEC, VMEM_SPEC, VMEM_SPEC, HBM_SPEC],
        out_specs=[VMEM_SPEC] * 2,
        scratch_shapes=[pltpu.SemaphoreType.DMA((capacity,))],
        compiler_params=params(4),
        cost_estimate=cost(last, capacity),
        name="last_exports",
    )(plan, psi_live, ahead, left)
    received.append(lax.ppermute(outgoing, "sec", swap))

    right_blocks = pltpu.VMEM((per_part, terms * rows, cols), BF16)
    right_sem = pltpu.SemaphoreType.DMA((per_part, terms))
    local_mixed, right_part = pl.pallas_call(
        local_kernel,
        out_shape=[blocks(capacity), right_blocks],
        in_specs=[SMEM_SPEC, VMEM_SPEC, VMEM_SPEC, HBM_SPEC],
        out_specs=[VMEM_SPEC] * 2,
        scratch_shapes=[right_sem],
        compiler_params=params(4),
        cost_estimate=cost(capacity, items),
        name="local_mixed",
    )(plan, psi_live, left_local, right)

    partners = partner_lists()
    kept, coming = [], []
    for part in range(PARTS):
        arrived = received if part else received[:1]
        ahead_of = part < PARTS - 1
        send, keep, *right_next = pl.pallas_call(
            functools.partial(part_kernel, part, ORDERS[part]),
            out_shape=[
                pltpu.VMEM((half, per_part * 8, cols), BF16),
                pltpu.VMEM((half, per_part * 8, cols), F32),
            ]
            + [right_blocks] * ahead_of,
            in_specs=[SMEM_SPEC] + [VMEM_SPEC] * (2 + len(arrived)) + [HBM_SPEC] * ahead_of,
            out_specs=[VMEM_SPEC] * (2 + ahead_of),
            scratch_shapes=[
                pltpu.VMEM((per_part,) + block, F32),
                pltpu.VMEM((per_part, rows, terms * rows), BF16),
            ]
            + [right_sem] * ahead_of,
            compiler_params=params(12),
            cost_estimate=cost(10 * part_items, part_items),
            name="part_sums",
        )(plan, local_mixed, *arrived, right_part, *[right] * ahead_of)
        right_part = right_next[0] if ahead_of else None
        kept.append(keep)
        coming.append(lax.ppermute(send, ("sec", "op"), partners[ORDERS[part][0]][0]))

    for step in range(1, 6):
        half //= 2
        for part in range(PARTS):
            keep, come = kept[part], coming[part]
            send = (keep[half:] + come[half:].astype(F32)).astype(BF16)
            kept[part] = keep[:half] + come[:half].astype(F32)
            axis = ORDERS[part][step // 2]
            coming[part] = lax.ppermute(send, ("sec", "op"), partners[axis][step % 2])
    done = [(keep + come.astype(F32)).astype(BF16) for keep, come in zip(kept, coming)]
    return jnp.concatenate([d.reshape(per_part, 8, cols) for d in done], axis=0)


def solution(mesh):
    placed = (
        P("sec", None, None),
        P("sec"),
        P("op", "sec", None, None),
        P("op", "sec", None, None),
        P("op", "sec"),
    )
    return jax.shard_map(
        per_device, mesh=mesh, in_specs=placed, out_specs=P("sec", "op", None), check_vma=False
    )
```

```python
import functools

import jax
import jax.numpy as jnp
from jax import lax
from jax.experimental import pallas as pl
from jax.experimental.pallas import tpu as pltpu
from jax.sharding import PartitionSpec as P

BF16, F32, I32 = jnp.bfloat16, jnp.float32, jnp.int32
PARTS = 3
PAD = 64
LIST, EXPORT, LOCAL, HERE, SLOT, PLAN = 32, 0, 64, 128, 160, 192
ORDERS = ((0, 1, 2), (1, 2, 0), (2, 0, 1))
STRIDES = (16, 4, 1)
SMEM_SPEC = pl.BlockSpec(memory_space=pltpu.SMEM)
VMEM_SPEC = pl.BlockSpec(memory_space=pltpu.VMEM)
ANY_SPEC = pl.BlockSpec(memory_space=pl.ANY)
HBM_SPEC = pl.BlockSpec(memory_space=pltpu.HBM)


def dot(a, b):
    return jnp.dot(a, b, preferred_element_type=F32)


def cleared(psi_live, j, live):
    rows, cols = psi_live.shape[1:]

    @pl.loop(live // PAD, rows // PAD)
    def _(n):
        psi_live[j, pl.ds(pl.multiple_of(n * PAD, PAD), PAD), :] = jnp.zeros((PAD, cols), BF16)


def waited(source, target, sem):
    @pl.loop(0, target.shape[0])
    def _(i):
        pltpu.make_async_copy(source.at[0, 0], target.at[i], sem.at[i]).wait()


def first_kernel(
    routes_in, live_in, psi, left, out, psi_live, ahead, plan, routes, live, inverse, state, left_buf,
    table_sem, psi_sem, left_sem, ahead_sem
):
    terms, slots = routes.shape
    me = lax.axis_index("sec")
    tables = (
        pltpu.make_async_copy(routes_in, routes, table_sem.at[0]),
        pltpu.make_async_copy(live_in, live, table_sem.at[1]),
    )
    for copy in tables:
        copy.start()

    def load_psi(j):
        return pltpu.make_async_copy(psi.at[j], psi_live.at[j], psi_sem.at[j])

    def want_psi(j):
        @pl.when(state[j] == 0)
        def _():
            load_psi(j).start()
            state[j] = 1

    def have_psi(j):
        @pl.when(state[j] == 1)
        def _():
            load_psi(j).wait()
            cleared(psi_live, j, live[j])
            state[j] = 2

    for j in range(slots):
        state[j] = 0

    for t in range(terms):
        for s in range(2 * slots):
            inverse[t, s] = -1
    for copy in tables:
        copy.wait()
    for t in range(terms):
        for j in range(slots):
            inverse[t, routes[t, j]] = j

    def listed(owner, at):
        count = jnp.int32(0)
        for s in range(slots):
            for t in range(terms):
                j = inverse[t, owner * slots + s]
                plan[at + count] = t
                plan[at + LIST + count] = j
                count = count + (j >= 0).astype(I32)
        for n in range(11, 13):
            plan[at + n] = jnp.where(n < count, plan[at + n], plan[at + 10])
            plan[at + LIST + n] = jnp.where(n < count, plan[at + LIST + n], plan[at + LIST + 10])

    first = out.shape[0]
    listed(1 - me, EXPORT)

    def load_left(i):
        source = left.at[plan[EXPORT + i], plan[EXPORT + LIST + i]]
        return pltpu.make_async_copy(source, left_buf.at[i], left_sem.at[i])

    @pl.loop(0, first)
    def _(i):
        want_psi(plan[EXPORT + LIST + i])
        load_left(i).start()

    @pl.loop(0, slots)
    def _(j):
        want_psi(j)

    listed(me, LOCAL)

    @pl.loop(0, ahead.shape[0])
    def _(i):
        at = EXPORT + first + i
        pltpu.make_async_copy(left.at[plan[at], plan[at + LIST]], ahead.at[i], ahead_sem.at[i]).start()

    local_count = jnp.int32(0)
    other_count = jnp.int32(0)
    for s in range(slots):
        for t in range(terms):
            here = (inverse[t, me * slots + s] >= 0).astype(I32)
            plan[HERE + terms * s + t] = here
            plan[SLOT + terms * s + t] = jnp.where(here == 1, local_count, other_count)
            local_count = local_count + here
            other_count = other_count + 1 - here
    for group in (range(first // 2), range(first // 2, first)):
        for i in group:
            have_psi(plan[EXPORT + LIST + i])
            load_left(i).wait()
        for i in group:
            out[i] = dot(left_buf[i], psi_live[plan[EXPORT + LIST + i]]).astype(BF16)
    for j in range(slots):
        have_psi(j)
    waited(left, ahead, ahead_sem)


def load_right(right, part, target, sem):
    terms, _, rows, _ = right.shape
    per_part = target.shape[0]

    def load(k, t):
        source = right.at[t, part * per_part + k]
        return pltpu.make_async_copy(source, target.at[k, pl.ds(rows * t, rows), :], sem.at[k, t])

    @pl.loop(0, per_part)
    def _(k):
        for t in range(terms):
            load(k, t).start()

    def wait():
        @pl.loop(0, per_part)
        def _(k):
            for t in range(terms):
                load(k, t).wait()

    return wait


def rest_kernel(plan, psi_live, ahead, left, right, out, local, right_part, left_buf, left_sem, right_sem):
    count = local.shape[0]

    def load_left(i):
        source = left.at[plan[LOCAL + i], plan[LOCAL + LIST + i]]
        return pltpu.make_async_copy(source, left_buf.at[i], left_sem.at[i])

    @pl.loop(0, count)
    def _(i):
        load_left(i).start()

    wait_right = load_right(right, 0, right_part, right_sem)
    skip = EXPORT + LIST + count - out.shape[0]
    for i in range(out.shape[0]):
        out[i] = dot(ahead[i], psi_live[plan[skip + i]]).astype(BF16)
    for group in (range(0, 6), range(6, count)):

        @pl.loop(group.start, group.stop)
        def _(i):
            load_left(i).wait()

        for i in group:
            local[i] = dot(left_buf[i], psi_live[plan[LOCAL + LIST + i]]).astype(BF16)
    wait_right()


def ring_places(c, core):
    near, far = c ^ 1, 3 - c
    return (c, jnp.where(core == 0, far, near), jnp.where(core == 0, near, far), c ^ 2)


def part_kernel(part, order, *refs):
    if part < PARTS - 1:
        plan, local_mixed, *received, right_part, right, send, keep, right_next, total, mixed, sem = refs
        wait = load_right(right, part + 1, right_next, sem)
    else:
        plan, local_mixed, *received, right_part, send, keep, total, mixed = refs
    per_part, rows, _ = total.shape
    terms = right_part.shape[1] // rows
    me = lax.axis_index("sec")
    op = lax.axis_index("op")
    place = (op // 16, (op // 4) % 4, op % 4)
    rings = [[8 * STRIDES[a] * spot for spot in ring_places(place[a], me)] for a in order]
    half = keep.shape[0]

    def block(s, t):
        here, slot = plan[HERE + terms * s + t], plan[SLOT + terms * s + t]
        last = received[0].shape[0] - 1
        came = received[0][jnp.minimum(slot, last)]
        if len(received) > 1:
            came = jnp.where(slot > last, received[1][jnp.clip(slot - last - 1, 0, received[1].shape[0] - 1)], came)
        return jnp.where(here == 1, local_mixed[slot], came)

    def product(k):
        s = part * per_part + k
        for t in range(terms):
            mixed[k, :, rows * t : rows * (t + 1)] = block(s, t)
        total[k] = dot(mixed[k], right_part[k])

    def lay_out(pair, numbers):
        for n in numbers:
            row = pl.multiple_of(rings[0][n // 16] + rings[1][n // 4 % 4] + rings[2][n % 4], 8)
            piece = jnp.concatenate([total[2 * pair + e, pl.ds(row, 8), :] for e in range(2)], axis=0)
            if n < half:
                keep[n, pl.ds(16 * pair, 16), :] = piece
            else:
                send[n - half, pl.ds(16 * pair, 16), :] = piece.astype(BF16)

    for k in range(per_part):
        product(k)
        if k > 1:
            lay_out(0, range(half * (k - 2), half * (k - 1)))
    lay_out(1, range(2 * half))
    if part < PARTS - 1:
        wait()


def partner_lists():
    lists = []
    for stride in STRIDES:
        pair = []
        for step in range(2):
            perm = []
            for core in range(2):
                for op in range(64):
                    c = op // stride % 4
                    d = c ^ 1 if core == step else 3 - c
                    perm.append((core * 64 + op, core * 64 + op + (d - c) * stride))
            pair.append(perm)
        lists.append(pair)
    return lists


def per_device(psi, live, left, right, routes):
    slots, rows, cols = psi.shape
    terms = left.shape[0]
    items = terms * slots
    capacity = items // 2 + 1
    per_part = slots // PARTS
    part_items = terms * per_part
    psi, live, left, right, routes = (
        pltpu.with_memory_space_constraint(x, pltpu.HBM) for x in (psi, live, left, right, routes)
    )
    block = (rows, cols)
    half = 32
    swap = [(0, 1), (1, 0)]
    flops = 2 * rows * rows * cols
    first, last = part_items, capacity - part_items

    def cost(dots, blocks):
        return pl.CostEstimate(flops=dots * flops, bytes_accessed=blocks * rows * cols * 2, transcendentals=0)

    def blocks(*count):
        return pltpu.VMEM(count + block, BF16)

    def params(mib):
        return pltpu.CompilerParams(vmem_limit_bytes=mib << 20)

    outgoing, psi_live, ahead, plan = pl.pallas_call(
        first_kernel,
        out_shape=[blocks(first), blocks(slots), blocks(last), pltpu.SMEM((PLAN,), I32)],
        in_specs=[HBM_SPEC] * 4,
        out_specs=[VMEM_SPEC] * 3 + [SMEM_SPEC],
        scratch_shapes=[
            pltpu.SMEM((terms, slots), I32),
            pltpu.SMEM((slots,), I32),
            pltpu.SMEM((terms, 2 * slots), I32),
            pltpu.SMEM((slots,), I32),
            blocks(first),
            pltpu.SemaphoreType.DMA((2,)),
            pltpu.SemaphoreType.DMA((slots,)),
            pltpu.SemaphoreType.DMA((first,)),
            pltpu.SemaphoreType.DMA((last,)),
        ],
        compiler_params=params(8),
        cost_estimate=cost(first, 2 * capacity),
        name="first_exports",
    )(routes, live, psi, left)
    received = [lax.ppermute(outgoing, "sec", swap)]

    right_blocks = pltpu.VMEM((per_part, terms * rows, cols), BF16)
    right_sem = pltpu.SemaphoreType.DMA((per_part, terms))
    outgoing, local_mixed, right_part = pl.pallas_call(
        rest_kernel,
        out_shape=[blocks(last), blocks(capacity), right_blocks],
        in_specs=[SMEM_SPEC, VMEM_SPEC, VMEM_SPEC, HBM_SPEC, HBM_SPEC],
        out_specs=[VMEM_SPEC] * 3,
        scratch_shapes=[blocks(capacity), pltpu.SemaphoreType.DMA((capacity,)), right_sem],
        compiler_params=params(12),
        cost_estimate=cost(last + capacity, capacity + part_items),
        name="rest_mixed",
    )(plan, psi_live, ahead, left, right)
    received.append(lax.ppermute(outgoing, "sec", swap))

    partners = partner_lists()
    kept, coming = [], []
    for part in range(PARTS):
        arrived = received if part else received[:1]
        ahead_of = part < PARTS - 1
        send, keep, *right_next = pl.pallas_call(
            functools.partial(part_kernel, part, ORDERS[part]),
            out_shape=[
                pltpu.VMEM((half, per_part * 8, cols), BF16),
                pltpu.VMEM((half, per_part * 8, cols), F32),
            ]
            + [right_blocks] * ahead_of,
            in_specs=[SMEM_SPEC] + [VMEM_SPEC] * (2 + len(arrived)) + [HBM_SPEC] * ahead_of,
            out_specs=[VMEM_SPEC] * (2 + ahead_of),
            scratch_shapes=[
                pltpu.VMEM((per_part,) + block, F32),
                pltpu.VMEM((per_part, rows, terms * rows), BF16),
            ]
            + [right_sem] * ahead_of,
            compiler_params=params(12),
            cost_estimate=cost(10 * part_items, part_items),
            name="part_sums",
        )(plan, local_mixed, *arrived, right_part, *[right] * ahead_of)
        right_part = right_next[0] if ahead_of else None
        kept.append(keep)
        coming.append(lax.ppermute(send, ("sec", "op"), partners[ORDERS[part][0]][0]))

    for step in range(1, 6):
        half //= 2
        for part in range(PARTS):
            keep, come = kept[part], coming[part]
            send = (keep[half:] + come[half:].astype(F32)).astype(BF16)
            kept[part] = keep[:half] + come[:half].astype(F32)
            axis = ORDERS[part][step // 2]
            coming[part] = lax.ppermute(send, ("sec", "op"), partners[axis][step % 2])
    out = jnp.zeros((slots, 8, cols), BF16)
    for part in range(PARTS):
        done = (kept[part] + coming[part].astype(F32)).astype(BF16).reshape(per_part, 8, cols)
        out = lax.dynamic_update_slice(out, done, (part * per_part, 0, 0))
    return out


def solution(mesh):
    placed = (
        P("sec", None, None),
        P("sec"),
        P("op", "sec", None, None),
        P("op", "sec", None, None),
        P("op", "sec"),
    )
    return jax.shard_map(
        per_device, mesh=mesh, in_specs=placed, out_specs=P("sec", "op", None), check_vma=False
    )
```

```python
import functools

import jax
import jax.numpy as jnp
from jax import lax
from jax.experimental import pallas as pl
from jax.experimental.pallas import tpu as pltpu
from jax.sharding import PartitionSpec as P

BF16, F32, I32 = jnp.bfloat16, jnp.float32, jnp.int32
PARTS = 3
PAD = 64
LIST, EXPORT, LOCAL, HERE, SLOT, PLAN = 32, 0, 64, 128, 160, 192
ORDERS = ((0, 1, 2), (1, 2, 0), (2, 0, 1))
STRIDES = (16, 4, 1)
SMEM_SPEC = pl.BlockSpec(memory_space=pltpu.SMEM)
VMEM_SPEC = pl.BlockSpec(memory_space=pltpu.VMEM)
ANY_SPEC = pl.BlockSpec(memory_space=pl.ANY)
HBM_SPEC = pl.BlockSpec(memory_space=pltpu.HBM)


def dot(a, b):
    return jnp.dot(a, b, preferred_element_type=F32)


def cleared(psi_live, j, live):
    rows, cols = psi_live.shape[1:]

    @pl.loop(live // PAD, rows // PAD)
    def _(n):
        psi_live[j, pl.ds(pl.multiple_of(n * PAD, PAD), PAD), :] = jnp.zeros((PAD, cols), BF16)


def waited(source, target, sem):
    @pl.loop(0, target.shape[0])
    def _(i):
        pltpu.make_async_copy(source.at[0, 0], target.at[i], sem.at[i]).wait()


def first_kernel(
    routes_in, live_in, psi, left, out, psi_live, ahead, plan, routes, live, inverse, state, left_buf,
    table_sem, psi_sem, left_sem, ahead_sem
):
    terms, slots = routes.shape
    me = lax.axis_index("sec")
    tables = (
        pltpu.make_async_copy(routes_in, routes, table_sem.at[0]),
        pltpu.make_async_copy(live_in, live, table_sem.at[1]),
    )
    for copy in tables:
        copy.start()

    def load_psi(j):
        return pltpu.make_async_copy(psi.at[j], psi_live.at[j], psi_sem.at[j])

    def want_psi(j):
        @pl.when(state[j] == 0)
        def _():
            load_psi(j).start()
            state[j] = 1

    def have_psi(j):
        @pl.when(state[j] == 1)
        def _():
            load_psi(j).wait()
            cleared(psi_live, j, live[j])
            state[j] = 2

    for j in range(slots):
        state[j] = 0

    for t in range(terms):
        for s in range(2 * slots):
            inverse[t, s] = -1
    for copy in tables:
        copy.wait()
    for t in range(terms):
        for j in range(slots):
            inverse[t, routes[t, j]] = j

    def listed(owner, at):
        count = jnp.int32(0)
        for s in range(slots):
            for t in range(terms):
                j = inverse[t, owner * slots + s]
                plan[at + count] = t
                plan[at + LIST + count] = j
                count = count + (j >= 0).astype(I32)
        for n in range(11, 13):
            plan[at + n] = jnp.where(n < count, plan[at + n], plan[at + 10])
            plan[at + LIST + n] = jnp.where(n < count, plan[at + LIST + n], plan[at + LIST + 10])

    first = out.shape[0]
    listed(1 - me, EXPORT)

    def load_left(i):
        source = left.at[plan[EXPORT + i], plan[EXPORT + LIST + i]]
        return pltpu.make_async_copy(source, left_buf.at[i], left_sem.at[i])

    @pl.loop(0, first)
    def _(i):
        want_psi(plan[EXPORT + LIST + i])
        load_left(i).start()

    @pl.loop(0, slots)
    def _(j):
        want_psi(j)

    listed(me, LOCAL)

    @pl.loop(0, ahead.shape[0])
    def _(i):
        at = EXPORT + first + i
        pltpu.make_async_copy(left.at[plan[at], plan[at + LIST]], ahead.at[i], ahead_sem.at[i]).start()

    local_count = jnp.int32(0)
    other_count = jnp.int32(0)
    for s in range(slots):
        for t in range(terms):
            here = (inverse[t, me * slots + s] >= 0).astype(I32)
            plan[HERE + terms * s + t] = here
            plan[SLOT + terms * s + t] = jnp.where(here == 1, local_count, other_count)
            local_count = local_count + here
            other_count = other_count + 1 - here
    for group in (range(2), range(2, 5), range(5, first)):
        for i in group:
            have_psi(plan[EXPORT + LIST + i])
            load_left(i).wait()
        for i in group:
            out[i] = dot(left_buf[i], psi_live[plan[EXPORT + LIST + i]]).astype(BF16)
    for j in range(slots):
        have_psi(j)
    waited(left, ahead, ahead_sem)


def load_right(right, part, target, sem):
    terms, _, rows, _ = right.shape
    per_part = target.shape[0]

    def load(k, t):
        source = right.at[t, part * per_part + k]
        return pltpu.make_async_copy(source, target.at[k, pl.ds(rows * t, rows), :], sem.at[k, t])

    @pl.loop(0, per_part)
    def _(k):
        for t in range(terms):
            load(k, t).start()

    def wait():
        @pl.loop(0, per_part)
        def _(k):
            for t in range(terms):
                load(k, t).wait()

    return wait


def rest_kernel(plan, psi_live, ahead, left, right, out, local, right_part, left_buf, left_sem, right_sem):
    count = local.shape[0]

    def load_left(i):
        source = left.at[plan[LOCAL + i], plan[LOCAL + LIST + i]]
        return pltpu.make_async_copy(source, left_buf.at[i], left_sem.at[i])

    @pl.loop(0, count)
    def _(i):
        load_left(i).start()

    wait_right = load_right(right, 0, right_part, right_sem)
    skip = EXPORT + LIST + count - out.shape[0]
    for i in range(out.shape[0]):
        out[i] = dot(ahead[i], psi_live[plan[skip + i]]).astype(BF16)
    for group in (range(0, 6), range(6, count)):

        @pl.loop(group.start, group.stop)
        def _(i):
            load_left(i).wait()

        for i in group:
            local[i] = dot(left_buf[i], psi_live[plan[LOCAL + LIST + i]]).astype(BF16)
    wait_right()


def ring_places(c, core):
    near, far = c ^ 1, 3 - c
    return (c, jnp.where(core == 0, far, near), jnp.where(core == 0, near, far), c ^ 2)


def part_kernel(part, order, *refs):
    if part < PARTS - 1:
        plan, local_mixed, *received, right_part, right, send, keep, right_next, total, mixed, sem = refs
        wait = load_right(right, part + 1, right_next, sem)
    else:
        plan, local_mixed, *received, right_part, send, keep, total, mixed = refs
    per_part, rows, _ = total.shape
    terms = right_part.shape[1] // rows
    me = lax.axis_index("sec")
    op = lax.axis_index("op")
    place = (op // 16, (op // 4) % 4, op % 4)
    rings = [[8 * STRIDES[a] * spot for spot in ring_places(place[a], me)] for a in order]
    half = keep.shape[0]

    def block(s, t):
        here, slot = plan[HERE + terms * s + t], plan[SLOT + terms * s + t]
        last = received[0].shape[0] - 1
        came = received[0][jnp.minimum(slot, last)]
        if len(received) > 1:
            came = jnp.where(slot > last, received[1][jnp.clip(slot - last - 1, 0, received[1].shape[0] - 1)], came)
        return jnp.where(here == 1, local_mixed[slot], came)

    def product(k):
        s = part * per_part + k
        for t in range(terms):
            mixed[k, :, rows * t : rows * (t + 1)] = block(s, t)
        total[k] = dot(mixed[k], right_part[k])

    def lay_out(pair, numbers):
        for n in numbers:
            row = pl.multiple_of(rings[0][n // 16] + rings[1][n // 4 % 4] + rings[2][n % 4], 8)
            piece = jnp.concatenate([total[2 * pair + e, pl.ds(row, 8), :] for e in range(2)], axis=0)
            if n < half:
                keep[n, pl.ds(16 * pair, 16), :] = piece
            else:
                send[n - half, pl.ds(16 * pair, 16), :] = piece.astype(BF16)

    for k in range(per_part):
        product(k)
        if k > 1:
            lay_out(0, range(half * (k - 2), half * (k - 1)))
    lay_out(1, range(2 * half))
    if part < PARTS - 1:
        wait()


def partner_lists():
    lists = []
    for stride in STRIDES:
        pair = []
        for step in range(2):
            perm = []
            for core in range(2):
                for op in range(64):
                    c = op // stride % 4
                    d = c ^ 1 if core == step else 3 - c
                    perm.append((core * 64 + op, core * 64 + op + (d - c) * stride))
            pair.append(perm)
        lists.append(pair)
    return lists


def per_device(psi, live, left, right, routes):
    slots, rows, cols = psi.shape
    terms = left.shape[0]
    items = terms * slots
    capacity = items // 2 + 1
    per_part = slots // PARTS
    part_items = terms * per_part
    psi, live, left, right, routes = (
        pltpu.with_memory_space_constraint(x, pltpu.HBM) for x in (psi, live, left, right, routes)
    )
    block = (rows, cols)
    half = 32
    swap = [(0, 1), (1, 0)]
    flops = 2 * rows * rows * cols
    first, last = part_items, capacity - part_items

    def cost(dots, blocks):
        return pl.CostEstimate(flops=dots * flops, bytes_accessed=blocks * rows * cols * 2, transcendentals=0)

    def blocks(*count):
        return pltpu.VMEM(count + block, BF16)

    def params(mib):
        return pltpu.CompilerParams(vmem_limit_bytes=mib << 20)

    outgoing, psi_live, ahead, plan = pl.pallas_call(
        first_kernel,
        out_shape=[blocks(first), blocks(slots), blocks(last), pltpu.SMEM((PLAN,), I32)],
        in_specs=[HBM_SPEC] * 4,
        out_specs=[VMEM_SPEC] * 3 + [SMEM_SPEC],
        scratch_shapes=[
            pltpu.SMEM((terms, slots), I32),
            pltpu.SMEM((slots,), I32),
            pltpu.SMEM((terms, 2 * slots), I32),
            pltpu.SMEM((slots,), I32),
            blocks(first),
            pltpu.SemaphoreType.DMA((2,)),
            pltpu.SemaphoreType.DMA((slots,)),
            pltpu.SemaphoreType.DMA((first,)),
            pltpu.SemaphoreType.DMA((last,)),
        ],
        compiler_params=params(8),
        cost_estimate=cost(first, 2 * capacity),
        name="first_exports",
    )(routes, live, psi, left)
    received = [lax.ppermute(outgoing, "sec", swap)]

    right_blocks = pltpu.VMEM((per_part, terms * rows, cols), BF16)
    right_sem = pltpu.SemaphoreType.DMA((per_part, terms))
    outgoing, local_mixed, right_part = pl.pallas_call(
        rest_kernel,
        out_shape=[blocks(last), blocks(capacity), right_blocks],
        in_specs=[SMEM_SPEC, VMEM_SPEC, VMEM_SPEC, HBM_SPEC, HBM_SPEC],
        out_specs=[VMEM_SPEC] * 3,
        scratch_shapes=[blocks(capacity), pltpu.SemaphoreType.DMA((capacity,)), right_sem],
        compiler_params=params(12),
        cost_estimate=cost(last + capacity, capacity + part_items),
        name="rest_mixed",
    )(plan, psi_live, ahead, left, right)
    received.append(lax.ppermute(outgoing, "sec", swap))

    partners = partner_lists()
    kept, coming = [], []
    for part in range(PARTS):
        arrived = received if part else received[:1]
        ahead_of = part < PARTS - 1
        send, keep, *right_next = pl.pallas_call(
            functools.partial(part_kernel, part, ORDERS[part]),
            out_shape=[
                pltpu.VMEM((half, per_part * 8, cols), BF16),
                pltpu.VMEM((half, per_part * 8, cols), F32),
            ]
            + [right_blocks] * ahead_of,
            in_specs=[SMEM_SPEC] + [VMEM_SPEC] * (2 + len(arrived)) + [HBM_SPEC] * ahead_of,
            out_specs=[VMEM_SPEC] * (2 + ahead_of),
            scratch_shapes=[
                pltpu.VMEM((per_part,) + block, F32),
                pltpu.VMEM((per_part, rows, terms * rows), BF16),
            ]
            + [right_sem] * ahead_of,
            compiler_params=params(12),
            cost_estimate=cost(10 * part_items, part_items),
            name="part_sums",
        )(plan, local_mixed, *arrived, right_part, *[right] * ahead_of)
        right_part = right_next[0] if ahead_of else None
        kept.append(keep)
        coming.append(lax.ppermute(send, ("sec", "op"), partners[ORDERS[part][0]][0]))

    for step in range(1, 6):
        half //= 2
        for part in range(PARTS):
            keep, come = kept[part], coming[part]
            send = (keep[half:] + come[half:].astype(F32)).astype(BF16)
            kept[part] = keep[:half] + come[:half].astype(F32)
            axis = ORDERS[part][step // 2]
            coming[part] = lax.ppermute(send, ("sec", "op"), partners[axis][step % 2])
    out = jnp.zeros((slots, 8, cols), BF16)
    for part in range(PARTS):
        done = (kept[part] + coming[part].astype(F32)).astype(BF16).reshape(per_part, 8, cols)
        out = lax.dynamic_update_slice(out, done, (part * per_part, 0, 0))
    return out


def solution(mesh):
    placed = (
        P("sec", None, None),
        P("sec"),
        P("op", "sec", None, None),
        P("op", "sec", None, None),
        P("op", "sec"),
    )
    return jax.shard_map(
        per_device, mesh=mesh, in_specs=placed, out_specs=P("sec", "op", None), check_vma=False
    )
```
